256 devices in a mesh: dp: 32 (over y, z), uly: 8 (over x, core).
Axes of the slice: x: 4, y: 4, z: 8, core: 2. Of those that a mesh axis runs over, the one named last changes fastest.
Arguments:
- q_video: bfloat16 [32, 1760, 2048], P('dp', 'uly'), may hold values from -6 to 6
- k_video: bfloat16 [32, 1760, 2048], P('dp', 'uly'), may hold values from -6 to 6
- v_video: bfloat16 [32, 1760, 2048], P('dp', 'uly'), may hold values from -6 to 6
- q_audio: bfloat16 [32, 320, 2048], P('dp', 'uly'), may hold values from -6 to 6
- k_audio: bfloat16 [32, 320, 2048], P('dp', 'uly'), may hold values from -6 to 6
- v_audio: bfloat16 [32, 320, 2048], P('dp', 'uly'), may hold values from -6 to 6
- x_video: bfloat16 [32, 1760, 3072], P('dp', 'uly'), may hold values from -3 to 3
- x_audio: bfloat16 [32, 320, 3072], P('dp', 'uly'), may hold values from -3 to 3
- out_video_w: bfloat16 [2048, 3072], P('uly', 'dp'), may hold values from -0.125 to 0.125
- out_audio_w: bfloat16 [2048, 3072], P('uly', 'dp'), may hold values from -0.125 to 0.125
- mod_video: bfloat16 [256, 3072], replicated, may hold values from -0.5 to 0.5
- mod_audio: bfloat16 [256, 3072], replicated, may hold values from -0.5 to 0.5
- slopes: float32 [16], replicated, may hold values from 0.02 to 2
- timesteps: int32 [16], replicated, may hold values from 0 to 999
- pair_ids: int32 [32], P('dp'), may hold values from 0 to 15, as said below
- offsets: int32 [32], P('dp'), may hold values from -160 to 160
Outputs:
- out_video: bfloat16 [32, 1760, 3072], P('dp', 'uly')
- out_audio: bfloat16 [32, 320, 3072], P('dp', 'uly')
The draws below stay inside these ranges and needn't reach their ends.
Inputs may be any that keep to these rules, and one draw needn't show every extreme that they name: `pair_ids`: each pair number is named by exactly two samples.
All inputs are finite; a program needn't handle non-finite values.
Results may differ from the reference program's by a relative error of at most 0.007.
Values may be sent and summed in bfloat16 or wider, within the bound.
No kernel may reach another device: no remote copies, remote signals or barrier semaphores. Data moves between devices by JAX's collectives and lax.ppermute only.
A program may use at most 192 MiB of HBM per device.

```python
import math
import jax
import jax.numpy as jnp
from jax import lax

D = 3072
HEADS = 16
HEAD_DIM = 128
FREQ = 256
NSTEPS = 1000
FRAME_TOK = 880
AUD_FRAME = 160
SAMPLES = 32
PAIRS = 16
VIDEO_LEN = 1760
AUDIO_LEN = 320
N_ULY = 8


def draw_q_video(key, part):
    key = jax.random.fold_in(key, 1)
    shape = (SAMPLES, VIDEO_LEN, HEADS * HEAD_DIM)
    values = jnp.clip(jax.random.normal(key, shape, jnp.float32), -6.0, 6.0)
    return values.astype(jnp.bfloat16)


def draw_k_video(key, part):
    key = jax.random.fold_in(key, 2)
    shape = (SAMPLES, VIDEO_LEN, HEADS * HEAD_DIM)
    values = jnp.clip(jax.random.normal(key, shape, jnp.float32), -6.0, 6.0)
    return values.astype(jnp.bfloat16)


def draw_q_audio(key, part):
    key = jax.random.fold_in(key, 3)
    shape = (SAMPLES, AUDIO_LEN, HEADS * HEAD_DIM)
    values = jnp.clip(jax.random.normal(key, shape, jnp.float32), -6.0, 6.0)
    return values.astype(jnp.bfloat16)


def draw_pair_ids(key, part):
    key = jax.random.fold_in(key, 5)
    return (jax.random.permutation(key, SAMPLES) // 2).astype(jnp.int32)


def place_ends(values, rng, smallest, high):
    longest = values.shape.index(max(values.shape))
    spots = []
    for shift in (0, 1):
        where = [jax.random.randint(jax.random.fold_in(rng, axis), (), 0, length) for axis, length in enumerate(values.shape)]
        where[longest] = (where[longest] + shift) % values.shape[longest]
        spots.append(tuple(where))
    return values.at[spots[0]].set(smallest).at[spots[1]].set(high)


def steps_of(key, extent, split, low, high):
    factor_of = 1.0
    for position, blocks in split:
        heights = jax.random.uniform(jax.random.fold_in(jax.random.fold_in(key, 6), position), (blocks,), jnp.float32, low / len(split), high / len(split))
        factor_of = factor_of * jnp.repeat(jnp.exp(heights), extent[position] // blocks).reshape((-1,) + (1,) * (len(extent) - 1 - position))
    return factor_of


def gaussian(stream_key, dims, spread, limit, pieces=(), held_as=jnp.bfloat16):
    values = spread * jax.random.normal(stream_key, dims, jnp.float32)
    if pieces:
        values = values * steps_of(stream_key, dims, pieces, -0.22, 0.18)
    return jnp.clip(values, -limit, limit).astype(held_as)


def setup_inputs(seed: int = 0) -> dict:
    streams_of = jax.random.split(jax.random.key(seed), 17)
    return {
        "q_video": draw_q_video(jax.random.fold_in(streams_of[16], 71), 0),
        "k_video": draw_k_video(jax.random.fold_in(streams_of[16], 71), 0),
        "v_video": gaussian(streams_of[2], (SAMPLES, VIDEO_LEN, HEADS * HEAD_DIM), 1.0, 6.0, ((0, 32), (1, 8))),
        "q_audio": draw_q_audio(jax.random.fold_in(streams_of[16], 71), 0),
        "k_audio": gaussian(streams_of[4], (SAMPLES, AUDIO_LEN, HEADS * HEAD_DIM), 1.0, 6.0, ((0, 32), (1, 8))),
        "v_audio": gaussian(streams_of[5], (SAMPLES, AUDIO_LEN, HEADS * HEAD_DIM), 1.0, 6.0, ((0, 32), (1, 8))),
        "x_video": gaussian(streams_of[6], (SAMPLES, VIDEO_LEN, D), 0.5, 3.0, ((0, 32), (1, 8))),
        "x_audio": gaussian(streams_of[7], (SAMPLES, AUDIO_LEN, D), 0.5, 3.0, ((0, 32), (1, 8))),
        "out_video_w": gaussian(streams_of[8], (HEADS * HEAD_DIM, D), (HEADS * HEAD_DIM) ** -0.5, 0.125, ((0, 8), (1, 32))),
        "out_audio_w": gaussian(streams_of[9], (HEADS * HEAD_DIM, D), (HEADS * HEAD_DIM) ** -0.5, 0.125, ((0, 8), (1, 32))),
        "mod_video": gaussian(streams_of[10], (FREQ, D), (FREQ // 2) ** -0.5, 0.5),
        "mod_audio": gaussian(streams_of[11], (FREQ, D), (FREQ // 2) ** -0.5, 0.5),
        "slopes": jnp.clip(jnp.exp(jax.random.uniform(streams_of[12], (HEADS,), jnp.float32, math.log(0.02), math.log(2.0))), 0.02, 2.0),
        "timesteps": place_ends(jax.random.randint(streams_of[13], (PAIRS,), 0, NSTEPS), jax.random.fold_in(streams_of[13], 1), 0, NSTEPS - 1).astype(jnp.int32),
        "pair_ids": draw_pair_ids(jax.random.fold_in(streams_of[16], 71), 0),
        "offsets": place_ends(jax.random.randint(streams_of[15], (SAMPLES,), 0 - AUD_FRAME, AUD_FRAME + 1), jax.random.fold_in(streams_of[15], 1), 0 - AUD_FRAME, AUD_FRAME).astype(jnp.int32),
    }


def attend_head(query, keys, values, query_time, key_time, slope):
    scores = jnp.dot(query, keys.T, preferred_element_type=jnp.float32) * (1.0 / math.sqrt(HEAD_DIM))
    scores = scores - slope * jnp.abs(query_time[:, None] - key_time[None, :])
    top = lax.optimization_barrier(jnp.max(scores, axis=1, keepdims=True))
    weights = jnp.exp(scores - top)
    total = lax.optimization_barrier(jnp.sum(weights, axis=1, keepdims=True))
    mixed = jnp.dot(weights.astype(jnp.bfloat16), values, preferred_element_type=jnp.float32)
    return (mixed / total).astype(jnp.bfloat16)

def timestep_embed(step_time):
    half = FREQ // 2
    index = jnp.arange(half, dtype=jnp.float32)
    freqs = jnp.exp(-math.log(10000.0) * index / half)
    angles = step_time * freqs
    return jnp.concatenate([jnp.cos(angles), jnp.sin(angles)]).astype(jnp.bfloat16)

def split_heads(array):
    return array.reshape(array.shape[0], HEADS, HEAD_DIM).transpose(1, 0, 2)

def join_heads(array):
    return array.transpose(1, 0, 2).reshape(array.shape[1], HEADS * HEAD_DIM)

def grouped_project(attn, weight):
    width = HEADS * HEAD_DIM // N_ULY
    total = jnp.zeros((attn.shape[0], weight.shape[1]), jnp.float32)
    for group in range(N_ULY):
        part = jnp.dot(attn[:, group * width:(group + 1) * width], weight[group * width:(group + 1) * width], preferred_element_type=jnp.float32).astype(jnp.bfloat16)
        total = total + lax.optimization_barrier(part).astype(jnp.float32)
    return total

def reference(q_video, k_video, v_video, q_audio, k_audio, v_audio, x_video, x_audio, out_video_w, out_audio_w, mod_video, mod_audio, slopes, timesteps, pair_ids, offsets):
    time_video = (jnp.arange(VIDEO_LEN, dtype=jnp.int32) // FRAME_TOK).astype(jnp.float32)

    def one_sample(index):
        time_audio = (jnp.arange(AUDIO_LEN, dtype=jnp.int32) + offsets[index]).astype(jnp.float32) / AUD_FRAME
        key_time = jnp.concatenate([time_video, time_audio])
        keys = jnp.concatenate([k_video[index], k_audio[index]], axis=0)
        values = jnp.concatenate([v_video[index], v_audio[index]], axis=0)

        def per_head(items):
            query_v, query_a, key_h, value_h, slope = items
            return (attend_head(query_v, key_h, value_h, time_video, key_time, slope), attend_head(query_a, key_h, value_h, time_audio, key_time, slope))
        attn_v, attn_a = lax.map(per_head, (split_heads(q_video[index]), split_heads(q_audio[index]), split_heads(keys), split_heads(values), slopes))
        attn_video = join_heads(attn_v)
        attn_audio = join_heads(attn_a)
        step_time = timesteps[pair_ids[index]].astype(jnp.float32)
        embed = timestep_embed(step_time)[None, :]
        gate_video = jnp.dot(embed, mod_video, preferred_element_type=jnp.float32)
        gate_audio = jnp.dot(embed, mod_audio, preferred_element_type=jnp.float32)
        proj_video = grouped_project(attn_video, out_video_w)
        proj_audio = grouped_project(attn_audio, out_audio_w)
        result_video = (x_video[index].astype(jnp.float32) + gate_video * proj_video).astype(jnp.bfloat16)
        result_audio = (x_audio[index].astype(jnp.float32) + gate_audio * proj_audio).astype(jnp.bfloat16)
        return (result_video, result_audio)
    out_video, out_audio = lax.map(one_sample, jnp.arange(SAMPLES, dtype=jnp.int32))
    return (out_video, out_audio)
```

```python
import functools
import math

import jax
import jax.numpy as jnp
from jax import lax
from jax.experimental import pallas as pl
from jax.experimental.pallas import tpu as pltpu
from jax.sharding import PartitionSpec as P

HEADS = 16
HEAD_DIM = 128
FREQ = 256
AUD_FRAME = 160
GROUPS = 8
XS, YS, ZS = 4, 4, 8
VID = 220
AUD = 40
VROWS = 224
AROWS = 48
ROWS = VROWS + AROWS
KEYS = GROUPS * ROWS
LOG2E = math.log2(math.e)
SCALE2 = LOG2E / math.sqrt(HEAD_DIM)
OUTSIDE = 1e30
VMEM = 60 * 2**20


def inner(left, right):
    return lax.dot_general(left, right, (((1,), (1,)), ((), ())), preferred_element_type=jnp.float32)


def pack_kernel(*refs):
    ins, outs = refs[:6], refs[6:]
    for head, out in enumerate(outs):
        for group in range(out.shape[0]):
            source = pl.ds((group * 2 + head) * HEAD_DIM, HEAD_DIM)
            for place in range(3):
                video, audio = ins[place], ins[place + 3]
                lanes = pl.ds(place * HEAD_DIM, HEAD_DIM)
                out[group, VROWS - 16 : VROWS, lanes] = jnp.zeros((16, HEAD_DIM), jnp.bfloat16)
                out[group, ROWS - 16 : ROWS, lanes] = jnp.zeros((16, HEAD_DIM), jnp.bfloat16)
                out[group, 0:VID, lanes] = video[0, :, source]
                out[group, VROWS : VROWS + AUD, lanes] = audio[0, :, source]


def pack(arrays):
    steps = 2
    width = arrays[0].shape[2] // steps
    video = pl.BlockSpec((1, VID, width), lambda g: (0, 0, g))
    audio = pl.BlockSpec((1, AUD, width), lambda g: (0, 0, g))
    out = pl.BlockSpec((GROUPS // steps, ROWS, 3 * HEAD_DIM), lambda g: (g, 0, 0))
    shape = jax.ShapeDtypeStruct((GROUPS, ROWS, 3 * HEAD_DIM), jnp.bfloat16)
    return pl.pallas_call(
        pack_kernel,
        grid=(steps,),
        in_specs=[video] * 3 + [audio] * 3,
        out_specs=[out, out],
        out_shape=[shape, shape],
        compiler_params=pltpu.CompilerParams(vmem_limit_bytes=VMEM),
        cost_estimate=pl.CostEstimate(flops=0, bytes_accessed=1_000_000, transcendentals=0),
    )(*arrays)


def weights_of(scores, bias):
    exponents = scores * SCALE2 - bias
    top = jnp.max(exponents, axis=1, keepdims=True)
    return jnp.exp2(exponents - top).astype(jnp.bfloat16)


def attend_kernel(chip, scalars, key_rows, query, keys, values, *refs):
    outs, out_audio, values_ones = refs[:-2], refs[-2], refs[-1]
    step = pl.program_id(0)
    first = lax.rem(chip[0] + step, XS) * 2

    @pl.when(step == 0)
    def _():
        values_ones[:, :HEAD_DIM] = values[...].reshape(KEYS, HEAD_DIM)
        values_ones[:, HEAD_DIM:] = jnp.ones((KEYS, HEAD_DIM), jnp.bfloat16)

    slope = scalars[0] * LOG2E
    offset = scalars[1]
    key_time = key_rows[0:1, :]
    outside = key_rows[1:2, :]
    all_keys = keys[...].reshape(KEYS, HEAD_DIM)

    def mix(part, query_time):
        bias = slope * jnp.abs(query_time - key_time) + outside
        sums = jnp.dot(
            weights_of(inner(part, all_keys), bias),
            values_ones[...],
            preferred_element_type=jnp.float32,
        )
        return (sums[:, :HEAD_DIM] / sums[:, HEAD_DIM:]).astype(jnp.bfloat16)

    video, times = [], []
    for side in range(2):
        block = first + side
        frame = (block // (GROUPS // 2)).astype(jnp.float32)
        video.append(mix(query[side, :VROWS, :], frame))
        index = lax.broadcasted_iota(jnp.int32, (AROWS, 1), 0) + block * AUD
        times.append((index.astype(jnp.float32) + offset) / AUD_FRAME)
    audio = mix(
        jnp.concatenate([query[side, VROWS:, :] for side in range(2)], axis=0),
        jnp.concatenate(times, axis=0),
    )
    for side in range(2):
        out_audio[first // 2, side] = audio[side * AROWS : (side + 1) * AROWS]
    for dx, out in enumerate(outs):

        @pl.when(step == dx)
        def _(out=out):
            for side in range(2):
                out[side] = video[side]


def attend(chip, scalars, key_rows, qkv):
    video = jax.ShapeDtypeStruct((2, VROWS, HEAD_DIM), jnp.bfloat16)
    return pl.pallas_call(
        attend_kernel,
        grid_spec=pltpu.PrefetchScalarGridSpec(
            num_scalar_prefetch=2,
            grid=(XS,),
            in_specs=[
                pl.BlockSpec((2, KEYS), lambda i, c, s: (0, 0)),
                pl.BlockSpec((2, ROWS, HEAD_DIM), lambda i, c, s: (lax.rem(c[0] + i, XS), 0, 0)),
                pl.BlockSpec((GROUPS, ROWS, HEAD_DIM), lambda i, c, s: (0, 0, 1)),
                pl.BlockSpec((GROUPS, ROWS, HEAD_DIM), lambda i, c, s: (0, 0, 2)),
            ],
            out_specs=[pl.BlockSpec((2, VROWS, HEAD_DIM), lambda i, c, s: (0, 0, 0))] * XS
            + [pl.BlockSpec((XS, 2, AROWS, HEAD_DIM), lambda i, c, s: (0, 0, 0, 0))],
            scratch_shapes=[pltpu.VMEM((KEYS, 2 * HEAD_DIM), jnp.bfloat16)],
        ),
        out_shape=[video] * XS
        + [jax.ShapeDtypeStruct((XS, 2, AROWS, HEAD_DIM), jnp.bfloat16)],
        compiler_params=pltpu.CompilerParams(vmem_limit_bytes=VMEM),
        cost_estimate=pl.CostEstimate(flops=0, bytes_accessed=1_000_000, transcendentals=0),
    )(chip, scalars, key_rows, qkv, qkv, qkv)


def audio_kernel(place, own, other, weight, out, left):
    chip, core = place[0], place[1]
    for half, source in enumerate((own, other)):
        side = core if half == 0 else 1 - core
        for dx in range(XS):
            group = lax.rem(chip - dx + XS, XS) * 2 + side
            for head in range(2):
                low = pl.multiple_of(group * 256 + head * HEAD_DIM, HEAD_DIM)
                left[:, pl.ds(low, HEAD_DIM)] = source[dx, head].reshape(
                    GROUPS * AROWS, HEAD_DIM
                )
    columns = out.shape[2]
    blocks = weight.shape[0] // GROUPS
    rows = [
        weight[group * blocks : (group + 1) * blocks, 0].reshape(columns, 256)
        for group in range(GROUPS)
    ]
    total = inner(left[...], jnp.concatenate(rows, axis=1))
    for device in range(GROUPS):
        out[device] = total[device * AROWS : device * AROWS + AUD].astype(jnp.bfloat16)


def project_audio(place, own, other, weights):
    blocks, slots, width, _ = weights.shape
    whole = pl.BlockSpec(own.shape, lambda n, p: (0,) * own.ndim)
    out = (GROUPS, AUD, blocks // GROUPS * width)
    return pl.pallas_call(
        audio_kernel,
        grid_spec=pltpu.PrefetchScalarGridSpec(
            num_scalar_prefetch=1,
            grid=(1,),
            in_specs=[
                whole,
                whole,
                pl.BlockSpec((blocks, 1, width, 256), lambda n, p: (0, slots - 1, 0, 0)),
            ],
            out_specs=pl.BlockSpec(out, lambda n, p: (0, 0, 0)),
            scratch_shapes=[pltpu.VMEM((GROUPS * AROWS, GROUPS * 256), jnp.bfloat16)],
        ),
        out_shape=jax.ShapeDtypeStruct(out, jnp.bfloat16),
        compiler_params=pltpu.CompilerParams(vmem_limit_bytes=VMEM),
        cost_estimate=pl.CostEstimate(flops=0, bytes_accessed=8_000_000, transcendentals=0),
    )(place, own, other, weights)


def project_kernel(core, *refs):
    sources, weight, own, other, left = refs[: 2 * XS], *refs[2 * XS :]

    @pl.when(pl.program_id(0) == 0)
    def _():
        for half in range(2):
            side = core[0] if half == 0 else 1 - core[0]
            for number, source in enumerate(sources):
                head, dx = divmod(number, XS)
                lanes = pl.ds(dx * 256 + head * HEAD_DIM, HEAD_DIM)
                left[half * VROWS : (half + 1) * VROWS, lanes] = source[side]

    columns = own.shape[1]
    rows = [weight[:, dx].reshape(columns, 256) for dx in range(XS)]
    total = inner(left[...], jnp.concatenate(rows, axis=1))
    own[...] = total[:VROWS].astype(jnp.bfloat16)
    other[...] = total[VROWS:].astype(jnp.bfloat16)


def project(core, sources, weights):
    blocks, _, width, _ = weights.shape
    step = ZS
    out = pl.BlockSpec((VROWS, step * width), lambda n, c: (0, n))
    shape = jax.ShapeDtypeStruct((VROWS, blocks * width), jnp.bfloat16)
    return pl.pallas_call(
        project_kernel,
        grid_spec=pltpu.PrefetchScalarGridSpec(
            num_scalar_prefetch=1,
            grid=(blocks // step,),
            in_specs=[pl.BlockSpec((2, VROWS, HEAD_DIM), lambda n, c: (0, 0, 0))] * (2 * XS)
            + [pl.BlockSpec((step, XS, width, 256), lambda n, c: (n, 0, 0, 0))],
            out_specs=[out, out],
            scratch_shapes=[pltpu.VMEM((2 * VROWS, XS * 256), jnp.bfloat16)],
        ),
        out_shape=[shape, shape],
        compiler_params=pltpu.CompilerParams(vmem_limit_bytes=VMEM),
        cost_estimate=pl.CostEstimate(flops=0, bytes_accessed=25_000_000, transcendentals=0),
    )(core, *sources, weights)


def along(array, axis, shift):
    if axis == "x":
        return lax.ppermute(array, "uly", [(i, (i + 2 * shift) % GROUPS) for i in range(GROUPS)])
    pairs = []
    for i in range(YS * ZS):
        row, column = divmod(i, ZS)
        if axis == "y":
            row = (row + shift) % YS
        else:
            column = (column + shift) % ZS
        pairs.append((i, row * ZS + column))
    return lax.ppermute(array, "dp", pairs)


def after(array, *others):
    return lax.optimization_barrier((array, *others))[0]


def video_kernel(own, other, x, gate, out):
    total = own[...].astype(jnp.float32) + other[...].astype(jnp.float32)
    out[0] = (x[0].astype(jnp.float32) + gate[...] * total[:VID]).astype(jnp.bfloat16)


def finish_video(own, other, x, gate):
    total = own.shape[1]
    step = total // 4
    half = pl.BlockSpec((VROWS, step), lambda n: (0, n))
    video = pl.BlockSpec((1, VID, step), lambda n: (0, 0, n))
    return pl.pallas_call(
        video_kernel,
        grid=(4,),
        in_specs=[half, half, video, pl.BlockSpec((1, step), lambda n: (0, n))],
        out_specs=video,
        out_shape=jax.ShapeDtypeStruct(x.shape, jnp.bfloat16),
        compiler_params=pltpu.CompilerParams(vmem_limit_bytes=VMEM // 4),
        cost_estimate=pl.CostEstimate(flops=0, bytes_accessed=6_000_000, transcendentals=0),
    )(own, other, x, gate)


def place_kernel(parts, x, gate, out):
    total = jnp.concatenate([parts[i] for i in range(GROUPS)], axis=1).astype(jnp.float32)
    out[0] = (x[0].astype(jnp.float32) + gate[...] * total).astype(jnp.bfloat16)


def finish_audio(parts, x, gate):
    return pl.pallas_call(
        place_kernel,
        out_shape=jax.ShapeDtypeStruct(x.shape, jnp.bfloat16),
        compiler_params=pltpu.CompilerParams(vmem_limit_bytes=VMEM // 4),
        cost_estimate=pl.CostEstimate(flops=0, bytes_accessed=3_000_000, transcendentals=0),
    )(parts, x, gate)


def timestep_embed(step_time):
    half = FREQ // 2
    index = jnp.arange(half, dtype=jnp.float32)
    freqs = jnp.exp(-math.log(10000.0) * index / half)
    angles = step_time * freqs
    return jnp.concatenate([jnp.cos(angles), jnp.sin(angles)]).astype(jnp.bfloat16)


def key_table(offset):
    index = jnp.arange(KEYS, dtype=jnp.int32)
    block, row = index // ROWS, index % ROWS
    is_video = row < VROWS
    video_time = (block // (GROUPS // 2)).astype(jnp.float32)
    audio_time = (block * AUD + (row - VROWS) + offset).astype(jnp.float32) / AUD_FRAME
    filling = (is_video & (row >= VID)) | (row >= VROWS + AUD)
    return jnp.stack(
        [jnp.where(is_video, video_time, audio_time), jnp.where(filling, OUTSIDE, 0.0)]
    ).astype(jnp.float32)


def shards(
    q_video,
    k_video,
    v_video,
    q_audio,
    k_audio,
    v_audio,
    x_video,
    x_audio,
    out_video_w,
    out_audio_w,
    mod_video,
    mod_audio,
    slopes,
    timesteps,
    pair_ids,
    offsets,
):
    position = lax.axis_index("uly")
    outer = lax.axis_index("dp")
    core = (position % 2).astype(jnp.int32)
    chip = (position // 2).astype(jnp.int32)
    own_heads = HEADS // GROUPS
    swap = [(i, i ^ 1) for i in range(GROUPS)]
    shifts = (1, 2, -1)

    block = out_video_w.T
    slots = [block] + [along(block, "x", shift) for shift in shifts]
    own_blocks = YS * ZS // GROUPS
    moves = []
    for column in range(YS * ZS):
        for group in range(GROUPS):
            over = group // 2 * ZS + group % 2 * own_blocks + column % own_blocks
            moves.append((column * GROUPS + group, over * GROUPS + column // own_blocks))
    slots.append(lax.ppermute(out_audio_w.T, ("dp", "uly"), moves))
    weights = lax.all_gather(jnp.stack(slots), "dp", axis=0, tiled=False)

    packed = pack((q_video, k_video, v_video, q_audio, k_audio, v_audio))
    qkv = [None, None]
    qkv[0] = lax.all_to_all(packed[0], "uly", split_axis=0, concat_axis=0, tiled=True)

    pair_count = timesteps.shape[0]
    step_time = jnp.sum(
        jnp.where(jnp.arange(pair_count, dtype=jnp.int32) == pair_ids[0], timesteps, 0)
    ).astype(jnp.float32)
    embed = timestep_embed(step_time)[None, :]
    gate_v = jnp.dot(embed, mod_video, preferred_element_type=jnp.float32)
    gate_a = jnp.dot(embed, mod_audio, preferred_element_type=jnp.float32)
    key_rows = key_table(offsets[0])
    offset = offsets[0].astype(jnp.float32)

    def attention(head, qkv):
        scalars = jnp.stack([slopes[position * own_heads + head], offset])
        *video, audio = attend(chip[None], scalars, key_rows, qkv)
        sent = [along(array, "x", dx) if dx else array for dx, array in enumerate(video)]
        return sent, audio, video[0]

    first, gate_v, gate_a, key_rows = lax.optimization_barrier((qkv[0], gate_v, gate_a, key_rows))
    qkv[1] = lax.all_to_all(
        after(packed[1], first), "uly", split_axis=0, concat_axis=0, tiled=True
    )
    sent0, audio0, done = attention(0, first)
    sent1, audio1, _ = attention(1, after(qkv[1], done))
    audio = jnp.stack([audio0, audio1])
    audio = jnp.stack([audio] + [along(audio, "x", shift) for shift in shifts])
    other_audio = lax.ppermute(audio, "uly", swap)
    parts = project_audio(jnp.stack([chip, core]), audio, other_audio, weights)
    sources = sent0 + sent1
    sources[0] = after(sources[0], parts)
    parts = lax.all_to_all(parts, "uly", split_axis=0, concat_axis=0, tiled=True)
    own, other = project(core[None], sources, weights)
    received = lax.ppermute(other, "uly", swap)
    out_audio = finish_audio(parts, x_audio, gate_a)
    return finish_video(own, received, x_video, gate_v), out_audio


def solution(mesh):
    tokens = P("dp", "uly", None)
    return jax.shard_map(
        shards,
        mesh=mesh,
        in_specs=(tokens,) * 8 + (P("uly", "dp"), P("uly", "dp")) + (P(),) * 4 + (P("dp"), P("dp")),
        out_specs=(tokens, tokens),
        check_vma=False,
    )
```

```python
import functools
import math

import jax
import jax.numpy as jnp
from jax import lax
from jax.experimental import pallas as pl
from jax.experimental.pallas import tpu as pltpu
from jax.sharding import PartitionSpec as P

HEADS = 16
HEAD_DIM = 128
FREQ = 256
AUD_FRAME = 160
GROUPS = 8
XS, YS, ZS = 4, 4, 8
VID = 220
AUD = 40
VROWS = 224
AROWS = 48
ROWS = VROWS + AROWS
KEYS = GROUPS * ROWS
MESSAGE = 2 * VROWS + GROUPS * AROWS
LOG2E = math.log2(math.e)
SCALE2 = LOG2E / math.sqrt(HEAD_DIM)
OUTSIDE = 1e30
VMEM = 60 * 2**20


def inner(left, right):
    return lax.dot_general(left, right, (((1,), (1,)), ((), ())), preferred_element_type=jnp.float32)


def pack_kernel(*refs):
    ins, outs = refs[:6], refs[6:]
    for head, out in enumerate(outs):
        for group in range(out.shape[0]):
            source = pl.ds((group * 2 + head) * HEAD_DIM, HEAD_DIM)
            for place in range(3):
                video, audio = ins[place], ins[place + 3]
                lanes = pl.ds(place * HEAD_DIM, HEAD_DIM)
                out[group, VROWS - 16 : VROWS, lanes] = jnp.zeros((16, HEAD_DIM), jnp.bfloat16)
                out[group, ROWS - 16 : ROWS, lanes] = jnp.zeros((16, HEAD_DIM), jnp.bfloat16)
                out[group, 0:VID, lanes] = video[0, :, source]
                out[group, VROWS : VROWS + AUD, lanes] = audio[0, :, source]


def pack(arrays):
    steps = 2
    width = arrays[0].shape[2] // steps
    video = pl.BlockSpec((1, VID, width), lambda g: (0, 0, g))
    audio = pl.BlockSpec((1, AUD, width), lambda g: (0, 0, g))
    out = pl.BlockSpec((GROUPS // steps, ROWS, 3 * HEAD_DIM), lambda g: (g, 0, 0))
    shape = jax.ShapeDtypeStruct((GROUPS, ROWS, 3 * HEAD_DIM), jnp.bfloat16)
    return pl.pallas_call(
        pack_kernel,
        grid=(steps,),
        in_specs=[video] * 3 + [audio] * 3,
        out_specs=[out, out],
        out_shape=[shape, shape],
        compiler_params=pltpu.CompilerParams(vmem_limit_bytes=VMEM),
        cost_estimate=pl.CostEstimate(flops=0, bytes_accessed=1_000_000, transcendentals=0),
    )(*arrays)


def weights_of(scores, bias):
    exponents = scores * SCALE2 - bias
    top = jnp.max(exponents, axis=1, keepdims=True)
    return jnp.exp2(exponents - top).astype(jnp.bfloat16)


def attend_kernel(chip, scalars, key_rows, query, keys, values, *refs):
    outs, values_ones = refs[:-1], refs[-1]
    step = pl.program_id(0)
    first = lax.rem(chip[0] + step, XS) * 2

    @pl.when(step == 0)
    def _():
        values_ones[:, :HEAD_DIM] = values[...].reshape(KEYS, HEAD_DIM)
        values_ones[:, HEAD_DIM:] = jnp.ones((KEYS, HEAD_DIM), jnp.bfloat16)

    slope = scalars[0] * LOG2E
    offset = scalars[1]
    key_time = key_rows[0:1, :]
    outside = key_rows[1:2, :]
    all_keys = keys[...].reshape(KEYS, HEAD_DIM)

    def mix(part, query_time):
        bias = slope * jnp.abs(query_time - key_time) + outside
        sums = jnp.dot(
            weights_of(inner(part, all_keys), bias),
            values_ones[...],
            preferred_element_type=jnp.float32,
        )
        return (sums[:, :HEAD_DIM] / sums[:, HEAD_DIM:]).astype(jnp.bfloat16)

    video, times = [], []
    for side in range(2):
        block = first + side
        frame = (block // (GROUPS // 2)).astype(jnp.float32)
        video.append(mix(query[side, :VROWS, :], frame))
        index = lax.broadcasted_iota(jnp.int32, (AROWS, 1), 0) + block * AUD
        times.append((index.astype(jnp.float32) + offset) / AUD_FRAME)
    audio = mix(
        jnp.concatenate([query[side, VROWS:, :] for side in range(2)], axis=0),
        jnp.concatenate(times, axis=0),
    )
    for dx, out in enumerate(outs):
        low = pl.multiple_of(2 * VROWS + first * AROWS, 16)
        out[pl.ds(low, 2 * AROWS), :] = audio

        @pl.when(step == dx)
        def _(out=out):
            for side in range(2):
                out[side * VROWS : (side + 1) * VROWS, :] = video[side]


def attend(chip, scalars, key_rows, qkv):
    message = jax.ShapeDtypeStruct((MESSAGE, HEAD_DIM), jnp.bfloat16)
    return pl.pallas_call(
        attend_kernel,
        grid_spec=pltpu.PrefetchScalarGridSpec(
            num_scalar_prefetch=2,
            grid=(XS,),
            in_specs=[
                pl.BlockSpec((2, KEYS), lambda i, c, s: (0, 0)),
                pl.BlockSpec((2, ROWS, HEAD_DIM), lambda i, c, s: (lax.rem(c[0] + i, XS), 0, 0)),
                pl.BlockSpec((GROUPS, ROWS, HEAD_DIM), lambda i, c, s: (0, 0, 1)),
                pl.BlockSpec((GROUPS, ROWS, HEAD_DIM), lambda i, c, s: (0, 0, 2)),
            ],
            out_specs=[pl.BlockSpec((MESSAGE, HEAD_DIM), lambda i, c, s: (0, 0))] * XS,
            scratch_shapes=[pltpu.VMEM((KEYS, 2 * HEAD_DIM), jnp.bfloat16)],
        ),
        out_shape=[message] * XS,
        compiler_params=pltpu.CompilerParams(vmem_limit_bytes=VMEM),
        cost_estimate=pl.CostEstimate(flops=0, bytes_accessed=1_000_000, transcendentals=0),
    )(chip, scalars, key_rows, qkv, qkv, qkv)


def audio_kernel(place, *refs):
    sources, weight, out, left = refs[: 2 * XS], *refs[2 * XS :]
    for number, source in enumerate(sources):
        head, dx = divmod(number, XS)
        low = lax.rem(place[0] - dx + XS, XS) * 256 + head * HEAD_DIM
        left[:, pl.ds(pl.multiple_of(low, HEAD_DIM), HEAD_DIM)] = source[2 * VROWS :, :]
    columns = out.shape[2]
    rows = [weight[x * ZS : (x + 1) * ZS, 0].reshape(columns, 256) for x in range(XS)]
    total = inner(left[...], jnp.concatenate(rows, axis=1))
    for device in range(GROUPS):
        out[device] = total[device * AROWS : device * AROWS + AUD].astype(jnp.bfloat16)


def project_audio(place, sources, weights):
    blocks, slots, width, _ = weights.shape
    out = (GROUPS, AUD, ZS * width)
    return pl.pallas_call(
        audio_kernel,
        grid_spec=pltpu.PrefetchScalarGridSpec(
            num_scalar_prefetch=1,
            grid=(1,),
            in_specs=[pl.BlockSpec((MESSAGE, HEAD_DIM), lambda n, p: (0, 0))] * (2 * XS)
            + [pl.BlockSpec((blocks, 1, width, 256), lambda n, p: (0, slots - 1, 0, 0))],
            out_specs=pl.BlockSpec(out, lambda n, p: (0, 0, 0)),
            scratch_shapes=[pltpu.VMEM((GROUPS * AROWS, XS * 256), jnp.bfloat16)],
        ),
        out_shape=jax.ShapeDtypeStruct(out, jnp.bfloat16),
        compiler_params=pltpu.CompilerParams(vmem_limit_bytes=VMEM),
        cost_estimate=pl.CostEstimate(flops=0, bytes_accessed=8_000_000, transcendentals=0),
    )(place, *sources, weights)


def project_kernel(place, *refs):
    sources, weight, own, other, left = refs[: 2 * XS], *refs[2 * XS :]

    @pl.when(pl.program_id(0) == 0)
    def _():
        for half in range(2):
            side = place[1] if half == 0 else 1 - place[1]
            low = pl.multiple_of(side * VROWS, 32)
            for number, source in enumerate(sources):
                head, dx = divmod(number, XS)
                lanes = pl.ds(dx * 256 + head * HEAD_DIM, HEAD_DIM)
                left[half * VROWS : (half + 1) * VROWS, lanes] = source[pl.ds(low, VROWS), :]

    columns = own.shape[1]
    rows = [weight[:, dx].reshape(columns, 256) for dx in range(XS)]
    total = inner(left[...], jnp.concatenate(rows, axis=1))
    own[...] = total[:VROWS].astype(jnp.bfloat16)
    other[...] = total[VROWS:].astype(jnp.bfloat16)


def project(place, sources, weights):
    width = weights.shape[2]
    step, count = ZS, YS
    out = pl.BlockSpec((VROWS, step * width), lambda n, p: (0, n))
    shape = jax.ShapeDtypeStruct((VROWS, count * step * width), jnp.bfloat16)
    return pl.pallas_call(
        project_kernel,
        grid_spec=pltpu.PrefetchScalarGridSpec(
            num_scalar_prefetch=1,
            grid=(count,),
            in_specs=[pl.BlockSpec((MESSAGE, HEAD_DIM), lambda n, p: (0, 0))] * (2 * XS)
            + [pl.BlockSpec((step, XS, width, 256), lambda n, p: (n, 0, 0, 0))],
            out_specs=[out, out],
            scratch_shapes=[pltpu.VMEM((2 * VROWS, XS * 256), jnp.bfloat16)],
        ),
        out_shape=[shape, shape],
        compiler_params=pltpu.CompilerParams(vmem_limit_bytes=VMEM),
        cost_estimate=pl.CostEstimate(
            flops=0, bytes_accessed=2_000_000 * count, transcendentals=0
        ),
    )(place, *sources, weights)


def along(array, axis, shift):
    if axis == "x":
        return lax.ppermute(array, "uly", [(i, (i + 2 * shift) % GROUPS) for i in range(GROUPS)])
    pairs = []
    for i in range(YS * ZS):
        row, column = divmod(i, ZS)
        if axis == "y":
            row = (row + shift) % YS
        else:
            column = (column + shift) % ZS
        pairs.append((i, row * ZS + column))
    return lax.ppermute(array, "dp", pairs)


def after(array, *others):
    return lax.optimization_barrier((array, *others))[0]


def video_kernel(own, other, x, gate, out):
    total = own[...].astype(jnp.float32) + other[...].astype(jnp.float32)
    out[0] = (x[0].astype(jnp.float32) + gate[...] * total[:VID]).astype(jnp.bfloat16)


def finish_video(own, other, x, gate):
    total = own.shape[1]
    step = total // 4
    half = pl.BlockSpec((VROWS, step), lambda n: (0, n))
    video = pl.BlockSpec((1, VID, step), lambda n: (0, 0, n))
    return pl.pallas_call(
        video_kernel,
        grid=(4,),
        in_specs=[half, half, video, pl.BlockSpec((1, step), lambda n: (0, n))],
        out_specs=video,
        out_shape=jax.ShapeDtypeStruct(x.shape, jnp.bfloat16),
        compiler_params=pltpu.CompilerParams(vmem_limit_bytes=VMEM // 4),
        cost_estimate=pl.CostEstimate(flops=0, bytes_accessed=6_000_000, transcendentals=0),
    )(own, other, x, gate)


def place_kernel(parts, x, gate, out):
    quarters = []
    for chip in range(XS):
        pair = parts[2 * chip].astype(jnp.float32) + parts[2 * chip + 1].astype(jnp.float32)
        quarters.append(pair)
    total = jnp.concatenate(quarters, axis=1)
    out[0] = (x[0].astype(jnp.float32) + gate[...] * total).astype(jnp.bfloat16)


def finish_audio(parts, x, gate):
    return pl.pallas_call(
        place_kernel,
        out_shape=jax.ShapeDtypeStruct(x.shape, jnp.bfloat16),
        compiler_params=pltpu.CompilerParams(vmem_limit_bytes=VMEM // 4),
        cost_estimate=pl.CostEstimate(flops=0, bytes_accessed=3_000_000, transcendentals=0),
    )(parts, x, gate)


def timestep_embed(step_time):
    half = FREQ // 2
    index = jnp.arange(half, dtype=jnp.float32)
    freqs = jnp.exp(-math.log(10000.0) * index / half)
    angles = step_time * freqs
    return jnp.concatenate([jnp.cos(angles), jnp.sin(angles)]).astype(jnp.bfloat16)


def key_table(offset):
    index = jnp.arange(KEYS, dtype=jnp.int32)
    block, row = index // ROWS, index % ROWS
    is_video = row < VROWS
    video_time = (block // (GROUPS // 2)).astype(jnp.float32)
    audio_time = (block * AUD + (row - VROWS) + offset).astype(jnp.float32) / AUD_FRAME
    filling = (is_video & (row >= VID)) | (row >= VROWS + AUD)
    return jnp.stack(
        [jnp.where(is_video, video_time, audio_time), jnp.where(filling, OUTSIDE, 0.0)]
    ).astype(jnp.float32)


def shards(
    q_video,
    k_video,
    v_video,
    q_audio,
    k_audio,
    v_audio,
    x_video,
    x_audio,
    out_video_w,
    out_audio_w,
    mod_video,
    mod_audio,
    slopes,
    timesteps,
    pair_ids,
    offsets,
):
    position = lax.axis_index("uly")
    outer = lax.axis_index("dp")
    core = (position % 2).astype(jnp.int32)
    chip = (position // 2).astype(jnp.int32)
    own_heads = HEADS // GROUPS
    swap = [(i, i ^ 1) for i in range(GROUPS)]
    shifts = (1, 2, -1)

    block = out_video_w.T
    near = [along(block, "x", shift) for shift in shifts]
    moves = []
    for over in range(YS * ZS):
        row, column = divmod(over, ZS)
        for group in range(GROUPS):
            target = (group // 2 * ZS + column) * GROUPS + row * 2 + group % 2
            moves.append((over * GROUPS + group, target))
    block_a = lax.ppermute(out_audio_w.T, ("dp", "uly"), moves)
    packed = pack((q_video, k_video, v_video, q_audio, k_audio, v_audio))
    block, *near = lax.optimization_barrier((block, *near, packed[0]))[:-1]
    weights = lax.all_gather(jnp.stack([block, *near, block_a]), "dp", axis=0, tiled=False)

    qkv = [None, None]
    qkv[0] = lax.all_to_all(packed[0], "uly", split_axis=0, concat_axis=0, tiled=True)

    pair_count = timesteps.shape[0]
    step_time = jnp.sum(
        jnp.where(jnp.arange(pair_count, dtype=jnp.int32) == pair_ids[0], timesteps, 0)
    ).astype(jnp.float32)
    embed = timestep_embed(step_time)[None, :]
    gate_v = jnp.dot(embed, mod_video, preferred_element_type=jnp.float32)
    gate_a = jnp.dot(embed, mod_audio, preferred_element_type=jnp.float32)
    key_rows = key_table(offsets[0])
    offset = offsets[0].astype(jnp.float32)

    def attention(head, qkv):
        scalars = jnp.stack([slopes[position * own_heads + head], offset])
        messages = attend(chip[None], scalars, key_rows, qkv)
        sent = [along(array, "x", dx) if dx else array for dx, array in enumerate(messages)]
        return sent, messages[0]

    first, gate_v, gate_a, key_rows = lax.optimization_barrier((qkv[0], gate_v, gate_a, key_rows))
    qkv[1] = lax.all_to_all(
        after(packed[1], first), "uly", split_axis=0, concat_axis=0, tiled=True
    )
    sent0, done = attention(0, first)
    sent1, _ = attention(1, after(qkv[1], done))
    place = jnp.stack([chip, core])
    sources = sent0 + sent1
    parts = project_audio(place, sources, weights)
    early = list(sources)
    early[0] = after(sources[0], parts)
    parts = lax.all_to_all(parts, "uly", split_axis=0, concat_axis=0, tiled=True)
    own, other = project(place, early, weights)
    other, parts = lax.optimization_barrier((other, parts))
    received = lax.ppermute(other, "uly", swap)
    out_audio = finish_audio(parts, x_audio, gate_a)
    return finish_video(own, received, x_video, gate_v), out_audio


def solution(mesh):
    tokens = P("dp", "uly", None)
    return jax.shard_map(
        shards,
        mesh=mesh,
        in_specs=(tokens,) * 8 + (P("uly", "dp"), P("uly", "dp")) + (P(),) * 4 + (P("dp"), P("dp")),
        out_specs=(tokens, tokens),
        check_vma=False,
    )
```

```python
import functools
import math

import jax
import jax.numpy as jnp
from jax import lax
from jax.experimental import pallas as pl
from jax.experimental.pallas import tpu as pltpu
from jax.sharding import PartitionSpec as P

HEADS = 16
HEAD_DIM = 128
FREQ = 256
AUD_FRAME = 160
GROUPS = 8
XS, YS, ZS = 4, 4, 8
VID = 220
AUD = 40
VROWS = 224
AROWS = 48
ROWS = VROWS + AROWS
KEYS = GROUPS * ROWS
MESSAGE = 2 * VROWS + GROUPS * AROWS
LOG2E = math.log2(math.e)
SCALE2 = LOG2E / math.sqrt(HEAD_DIM)
OUTSIDE = 1e30
VMEM = 60 * 2**20


def inner(left, right):
    return lax.dot_general(left, right, (((1,), (1,)), ((), ())), preferred_element_type=jnp.float32)


def pack_kernel(*refs):
    ins, outs = refs[:6], refs[6:]
    for head, out in enumerate(outs):
        for group in range(out.shape[0]):
            source = pl.ds((group * 2 + head) * HEAD_DIM, HEAD_DIM)
            for place in range(3):
                video, audio = ins[place], ins[place + 3]
                lanes = pl.ds(place * HEAD_DIM, HEAD_DIM)
                out[group, VROWS - 16 : VROWS, lanes] = jnp.zeros((16, HEAD_DIM), jnp.bfloat16)
                out[group, ROWS - 16 : ROWS, lanes] = jnp.zeros((16, HEAD_DIM), jnp.bfloat16)
                out[group, 0:VID, lanes] = video[0, :, source]
                out[group, VROWS : VROWS + AUD, lanes] = audio[0, :, source]


def pack(arrays):
    steps = 2
    width = arrays[0].shape[2] // steps
    video = pl.BlockSpec((1, VID, width), lambda g: (0, 0, g))
    audio = pl.BlockSpec((1, AUD, width), lambda g: (0, 0, g))
    out = pl.BlockSpec((GROUPS // steps, ROWS, 3 * HEAD_DIM), lambda g: (g, 0, 0))
    shape = jax.ShapeDtypeStruct((GROUPS, ROWS, 3 * HEAD_DIM), jnp.bfloat16)
    return pl.pallas_call(
        pack_kernel,
        grid=(steps,),
        in_specs=[video] * 3 + [audio] * 3,
        out_specs=[out, out],
        out_shape=[shape, shape],
        compiler_params=pltpu.CompilerParams(vmem_limit_bytes=VMEM),
        cost_estimate=pl.CostEstimate(flops=0, bytes_accessed=1_000_000, transcendentals=0),
    )(*arrays)


def weights_of(scores, bias):
    exponents = scores * SCALE2 - bias
    top = jnp.max(exponents, axis=1, keepdims=True)
    return jnp.exp2(exponents - top).astype(jnp.bfloat16)


def attend_kernel(chip, scalars, key_rows, query, keys, values, *refs):
    outs, values_ones = refs[:-1], refs[-1]
    step = pl.program_id(0)
    first = lax.rem(chip[0] + step, XS) * 2

    @pl.when(step == 0)
    def _():
        values_ones[:, :HEAD_DIM] = values[...].reshape(KEYS, HEAD_DIM)
        values_ones[:, HEAD_DIM:] = jnp.ones((KEYS, HEAD_DIM), jnp.bfloat16)

    slope = scalars[0] * LOG2E
    offset = scalars[1]
    key_time = key_rows[0:1, :]
    outside = key_rows[1:2, :]
    all_keys = keys[...].reshape(KEYS, HEAD_DIM)

    def mix(part, query_time):
        bias = slope * jnp.abs(query_time - key_time) + outside
        sums = jnp.dot(
            weights_of(inner(part, all_keys), bias),
            values_ones[...],
            preferred_element_type=jnp.float32,
        )
        return (sums[:, :HEAD_DIM] / sums[:, HEAD_DIM:]).astype(jnp.bfloat16)

    video, times = [], []
    for side in range(2):
        block = first + side
        frame = (block // (GROUPS // 2)).astype(jnp.float32)
        video.append(mix(query[side, :VROWS, :], frame))
        index = lax.broadcasted_iota(jnp.int32, (AROWS, 1), 0) + block * AUD
        times.append((index.astype(jnp.float32) + offset) / AUD_FRAME)
    audio = mix(
        jnp.concatenate([query[side, VROWS:, :] for side in range(2)], axis=0),
        jnp.concatenate(times, axis=0),
    )
    for dx, out in enumerate(outs):
        low = pl.multiple_of(2 * VROWS + first * AROWS, 16)
        out[pl.ds(low, 2 * AROWS), :] = audio

        @pl.when(step == dx)
        def _(out=out):
            for side in range(2):
                out[side * VROWS : (side + 1) * VROWS, :] = video[side]


def attend(chip, scalars, key_rows, qkv):
    message = jax.ShapeDtypeStruct((MESSAGE, HEAD_DIM), jnp.bfloat16)
    return pl.pallas_call(
        attend_kernel,
        grid_spec=pltpu.PrefetchScalarGridSpec(
            num_scalar_prefetch=2,
            grid=(XS,),
            in_specs=[
                pl.BlockSpec((2, KEYS), lambda i, c, s: (0, 0)),
                pl.BlockSpec((2, ROWS, HEAD_DIM), lambda i, c, s: (lax.rem(c[0] + i, XS), 0, 0)),
                pl.BlockSpec((GROUPS, ROWS, HEAD_DIM), lambda i, c, s: (0, 0, 1)),
                pl.BlockSpec((GROUPS, ROWS, HEAD_DIM), lambda i, c, s: (0, 0, 2)),
            ],
            out_specs=[pl.BlockSpec((MESSAGE, HEAD_DIM), lambda i, c, s: (0, 0))] * XS,
            scratch_shapes=[pltpu.VMEM((KEYS, 2 * HEAD_DIM), jnp.bfloat16)],
        ),
        out_shape=[message] * XS,
        compiler_params=pltpu.CompilerParams(vmem_limit_bytes=VMEM),
        cost_estimate=pl.CostEstimate(flops=0, bytes_accessed=1_000_000, transcendentals=0),
    )(chip, scalars, key_rows, qkv, qkv, qkv)


def gather_kernel(place, *refs):
    sources, video, audio = refs[: 2 * XS], refs[2 * XS], refs[2 * XS + 1]
    for number, source in enumerate(sources):
        head, dx = divmod(number, XS)
        lanes = pl.ds(dx * 256 + head * HEAD_DIM, HEAD_DIM)
        for half in range(2):
            side = place[1] if half == 0 else 1 - place[1]
            low = pl.multiple_of(side * VROWS, 32)
            video[half * VROWS : (half + 1) * VROWS, lanes] = source[pl.ds(low, VROWS), :]
        low = lax.rem(place[0] - dx + XS, XS) * 256 + head * HEAD_DIM
        audio[:, pl.ds(pl.multiple_of(low, HEAD_DIM), HEAD_DIM)] = source[2 * VROWS :, :]


def gather_rows(place, sources):
    whole = pl.BlockSpec(memory_space=pltpu.VMEM)
    return pl.pallas_call(
        gather_kernel,
        in_specs=[pl.BlockSpec(memory_space=pltpu.SMEM)] + [whole] * (2 * XS),
        out_specs=[whole, whole],
        out_shape=[
            jax.ShapeDtypeStruct((2 * VROWS, XS * 256), jnp.bfloat16),
            jax.ShapeDtypeStruct((GROUPS * AROWS, XS * 256), jnp.bfloat16),
        ],
        compiler_params=pltpu.CompilerParams(vmem_limit_bytes=VMEM),
        cost_estimate=pl.CostEstimate(flops=0, bytes_accessed=4_000_000, transcendentals=0),
    )(place, *sources)


def audio_kernel(left, weight, out):
    columns = out.shape[2]
    rows = [weight[x * ZS : (x + 1) * ZS, 0].reshape(columns, 256) for x in range(XS)]
    total = inner(left[...], jnp.concatenate(rows, axis=1))
    for device in range(GROUPS):
        out[device] = total[device * AROWS : device * AROWS + AUD].astype(jnp.bfloat16)


def project_audio(left, weights):
    blocks, slots, width, _ = weights.shape
    out = (GROUPS, AUD, ZS * width)
    return pl.pallas_call(
        audio_kernel,
        grid=(1,),
        in_specs=[
            pl.BlockSpec(left.shape, lambda n: (0, 0)),
            pl.BlockSpec((blocks, 1, width, 256), lambda n: (0, slots - 1, 0, 0)),
        ],
        out_specs=pl.BlockSpec(out, lambda n: (0, 0, 0)),
        out_shape=jax.ShapeDtypeStruct(out, jnp.bfloat16),
        compiler_params=pltpu.CompilerParams(vmem_limit_bytes=VMEM),
        cost_estimate=pl.CostEstimate(flops=0, bytes_accessed=8_000_000, transcendentals=0),
    )(left, weights)


def project_kernel(left, weight, own, other):
    columns = own.shape[1]
    rows = [weight[:, dx].reshape(columns, 256) for dx in range(XS)]
    total = inner(left[...], jnp.concatenate(rows, axis=1))
    own[...] = total[:VROWS].astype(jnp.bfloat16)
    other[...] = total[VROWS:].astype(jnp.bfloat16)


def project(left, weights):
    width = weights.shape[2]
    step, count = ZS, YS
    out = pl.BlockSpec((VROWS, step * width), lambda n: (0, n))
    shape = jax.ShapeDtypeStruct((VROWS, count * step * width), jnp.bfloat16)
    return pl.pallas_call(
        project_kernel,
        grid=(count,),
        in_specs=[
            pl.BlockSpec(left.shape, lambda n: (0, 0)),
            pl.BlockSpec((step, XS, width, 256), lambda n: (n, 0, 0, 0)),
        ],
        out_specs=[out, out],
        out_shape=[shape, shape],
        compiler_params=pltpu.CompilerParams(vmem_limit_bytes=VMEM),
        cost_estimate=pl.CostEstimate(flops=0, bytes_accessed=8_000_000, transcendentals=0),
    )(left, weights)


def along(array, axis, shift):
    if axis == "x":
        return lax.ppermute(array, "uly", [(i, (i + 2 * shift) % GROUPS) for i in range(GROUPS)])
    pairs = []
    for i in range(YS * ZS):
        row, column = divmod(i, ZS)
        if axis == "y":
            row = (row + shift) % YS
        else:
            column = (column + shift) % ZS
        pairs.append((i, row * ZS + column))
    return lax.ppermute(array, "dp", pairs)


def after(array, *others):
    return lax.optimization_barrier((array, *others))[0]


def video_kernel(own, other, x, gate, out):
    total = own[...].astype(jnp.float32) + other[...].astype(jnp.float32)
    out[0] = (x[0].astype(jnp.float32) + gate[...] * total[:VID]).astype(jnp.bfloat16)


def finish_video(own, other, x, gate):
    total = own.shape[1]
    step = total // 4
    half = pl.BlockSpec((VROWS, step), lambda n: (0, n))
    video = pl.BlockSpec((1, VID, step), lambda n: (0, 0, n))
    return pl.pallas_call(
        video_kernel,
        grid=(4,),
        in_specs=[half, half, video, pl.BlockSpec((1, step), lambda n: (0, n))],
        out_specs=video,
        out_shape=jax.ShapeDtypeStruct(x.shape, jnp.bfloat16),
        compiler_params=pltpu.CompilerParams(vmem_limit_bytes=VMEM // 4),
        cost_estimate=pl.CostEstimate(flops=0, bytes_accessed=6_000_000, transcendentals=0),
    )(own, other, x, gate)


def place_kernel(parts, x, gate, out):
    quarters = []
    for chip in range(XS):
        pair = parts[2 * chip].astype(jnp.float32) + parts[2 * chip + 1].astype(jnp.float32)
        quarters.append(pair)
    total = jnp.concatenate(quarters, axis=1)
    out[0] = (x[0].astype(jnp.float32) + gate[...] * total).astype(jnp.bfloat16)


def finish_audio(parts, x, gate):
    return pl.pallas_call(
        place_kernel,
        out_shape=jax.ShapeDtypeStruct(x.shape, jnp.bfloat16),
        compiler_params=pltpu.CompilerParams(vmem_limit_bytes=VMEM // 4),
        cost_estimate=pl.CostEstimate(flops=0, bytes_accessed=3_000_000, transcendentals=0),
    )(parts, x, gate)


def timestep_embed(step_time):
    half = FREQ // 2
    index = jnp.arange(half, dtype=jnp.float32)
    freqs = jnp.exp(-math.log(10000.0) * index / half)
    angles = step_time * freqs
    return jnp.concatenate([jnp.cos(angles), jnp.sin(angles)]).astype(jnp.bfloat16)


def key_table(offset):
    index = jnp.arange(KEYS, dtype=jnp.int32)
    block, row = index // ROWS, index % ROWS
    is_video = row < VROWS
    video_time = (block // (GROUPS // 2)).astype(jnp.float32)
    audio_time = (block * AUD + (row - VROWS) + offset).astype(jnp.float32) / AUD_FRAME
    filling = (is_video & (row >= VID)) | (row >= VROWS + AUD)
    return jnp.stack(
        [jnp.where(is_video, video_time, audio_time), jnp.where(filling, OUTSIDE, 0.0)]
    ).astype(jnp.float32)


def shards(
    q_video,
    k_video,
    v_video,
    q_audio,
    k_audio,
    v_audio,
    x_video,
    x_audio,
    out_video_w,
    out_audio_w,
    mod_video,
    mod_audio,
    slopes,
    timesteps,
    pair_ids,
    offsets,
):
    position = lax.axis_index("uly")
    outer = lax.axis_index("dp")
    core = (position % 2).astype(jnp.int32)
    chip = (position // 2).astype(jnp.int32)
    own_heads = HEADS // GROUPS
    swap = [(i, i ^ 1) for i in range(GROUPS)]
    shifts = (1, 2, -1)

    block = out_video_w.T
    near = [along(block, "x", shift) for shift in shifts]
    moves = []
    for over in range(YS * ZS):
        row, column = divmod(over, ZS)
        for group in range(GROUPS):
            target = (group // 2 * ZS + column) * GROUPS + row * 2 + group % 2
            moves.append((over * GROUPS + group, target))
    block_a = lax.ppermute(out_audio_w.T, ("dp", "uly"), moves)
    packed = pack((q_video, k_video, v_video, q_audio, k_audio, v_audio))
    block, *near = lax.optimization_barrier((block, *near, packed[0]))[:-1]
    weights = lax.all_gather(jnp.stack([block, *near, block_a]), "dp", axis=0, tiled=False)

    qkv = [None, None]
    qkv[0] = lax.all_to_all(packed[0], "uly", split_axis=0, concat_axis=0, tiled=True)

    pair_count = timesteps.shape[0]
    step_time = jnp.sum(
        jnp.where(jnp.arange(pair_count, dtype=jnp.int32) == pair_ids[0], timesteps, 0)
    ).astype(jnp.float32)
    embed = timestep_embed(step_time)[None, :]
    gate_v = jnp.dot(embed, mod_video, preferred_element_type=jnp.float32)
    gate_a = jnp.dot(embed, mod_audio, preferred_element_type=jnp.float32)
    key_rows = key_table(offsets[0])
    offset = offsets[0].astype(jnp.float32)

    def attention(head, qkv):
        scalars = jnp.stack([slopes[position * own_heads + head], offset])
        messages = attend(chip[None], scalars, key_rows, qkv)
        sent = [along(array, "x", dx) if dx else array for dx, array in enumerate(messages)]
        return sent, messages[0]

    first, gate_v, gate_a, key_rows = lax.optimization_barrier((qkv[0], gate_v, gate_a, key_rows))
    qkv[1] = lax.all_to_all(
        after(packed[1], first), "uly", split_axis=0, concat_axis=0, tiled=True
    )
    sent0, done = attention(0, first)
    sent1, _ = attention(1, after(qkv[1], done))
    place = jnp.stack([chip, core])
    left_v, left_a = gather_rows(place, sent0 + sent1)
    parts = project_audio(left_a, weights)
    left_v = after(left_v, parts)
    parts = lax.all_to_all(parts, "uly", split_axis=0, concat_axis=0, tiled=True)
    own, other = project(left_v, weights)
    other, parts = lax.optimization_barrier((other, parts))
    received = lax.ppermute(other, "uly", swap)
    out_audio = finish_audio(parts, x_audio, gate_a)
    return finish_video(own, received, x_video, gate_v), out_audio


def solution(mesh):
    tokens = P("dp", "uly", None)
    return jax.shard_map(
        shards,
        mesh=mesh,
        in_specs=(tokens,) * 8 + (P("uly", "dp"), P("uly", "dp")) + (P(),) * 4 + (P("dp"), P("dp")),
        out_specs=(tokens, tokens),
        check_vma=False,
    )
```

```python
import functools
import math

import jax
import jax.numpy as jnp
from jax import lax
from jax.experimental import pallas as pl
from jax.experimental.pallas import tpu as pltpu
from jax.sharding import PartitionSpec as P

HEADS = 16
HEAD_DIM = 128
FREQ = 256
AUD_FRAME = 160
GROUPS = 8
XS, YS, ZS = 4, 4, 8
VID = 220
AUD = 40
VROWS = 224
AROWS = 48
ROWS = VROWS + AROWS
KEYS = GROUPS * ROWS
MESSAGE = 2 * VROWS + GROUPS * AROWS
LOG2E = math.log2(math.e)
SCALE2 = LOG2E / math.sqrt(HEAD_DIM)
OUTSIDE = 1e30
VMEM = 60 * 2**20


def inner(left, right):
    return lax.dot_general(left, right, (((1,), (1,)), ((), ())), preferred_element_type=jnp.float32)


def pack_kernel(*refs):
    ins, outs = refs[:6], refs[6:]
    for head, out in enumerate(outs):
        for group in range(out.shape[0]):
            source = pl.ds((group * 2 + head) * HEAD_DIM, HEAD_DIM)
            for place in range(3):
                video, audio = ins[place], ins[place + 3]
                lanes = pl.ds(place * HEAD_DIM, HEAD_DIM)
                out[group, VROWS - 16 : VROWS, lanes] = jnp.zeros((16, HEAD_DIM), jnp.bfloat16)
                out[group, ROWS - 16 : ROWS, lanes] = jnp.zeros((16, HEAD_DIM), jnp.bfloat16)
                out[group, 0:VID, lanes] = video[0, :, source]
                out[group, VROWS : VROWS + AUD, lanes] = audio[0, :, source]


def pack(arrays):
    steps = 2
    width = arrays[0].shape[2] // steps
    video = pl.BlockSpec((1, VID, width), lambda g: (0, 0, g))
    audio = pl.BlockSpec((1, AUD, width), lambda g: (0, 0, g))
    out = pl.BlockSpec((GROUPS // steps, ROWS, 3 * HEAD_DIM), lambda g: (g, 0, 0))
    shape = jax.ShapeDtypeStruct((GROUPS, ROWS, 3 * HEAD_DIM), jnp.bfloat16)
    return pl.pallas_call(
        pack_kernel,
        grid=(steps,),
        in_specs=[video] * 3 + [audio] * 3,
        out_specs=[out, out],
        out_shape=[shape, shape],
        compiler_params=pltpu.CompilerParams(vmem_limit_bytes=VMEM),
        cost_estimate=pl.CostEstimate(flops=0, bytes_accessed=1_000_000, transcendentals=0),
    )(*arrays)


def weights_of(scores, bias):
    exponents = scores * SCALE2 - bias
    top = jnp.max(exponents, axis=1, keepdims=True)
    return jnp.exp2(exponents - top).astype(jnp.bfloat16)


def attend_kernel(chip, scalars, key_rows, query, keys, values, *refs):
    outs, values_ones = refs[:-1], refs[-1]
    step = pl.program_id(0)
    first = lax.rem(chip[0] + step, XS) * 2

    @pl.when(step == 0)
    def _():
        values_ones[:, :HEAD_DIM] = values[...].reshape(KEYS, HEAD_DIM)
        values_ones[:, HEAD_DIM:] = jnp.ones((KEYS, HEAD_DIM), jnp.bfloat16)

    slope = scalars[0] * LOG2E
    offset = scalars[1]
    key_time = key_rows[0:1, :]
    outside = key_rows[1:2, :]
    all_keys = keys[...].reshape(KEYS, HEAD_DIM)

    def mix(part, query_time):
        bias = slope * jnp.abs(query_time - key_time) + outside
        sums = jnp.dot(
            weights_of(inner(part, all_keys), bias),
            values_ones[...],
            preferred_element_type=jnp.float32,
        )
        return (sums[:, :HEAD_DIM] / sums[:, HEAD_DIM:]).astype(jnp.bfloat16)

    video, times = [], []
    for side in range(2):
        block = first + side
        frame = (block // (GROUPS // 2)).astype(jnp.float32)
        video.append(mix(query[side, :VROWS, :], frame))
        index = lax.broadcasted_iota(jnp.int32, (AROWS, 1), 0) + block * AUD
        times.append((index.astype(jnp.float32) + offset) / AUD_FRAME)
    audio = mix(
        jnp.concatenate([query[side, VROWS:, :] for side in range(2)], axis=0),
        jnp.concatenate(times, axis=0),
    )
    for dx, out in enumerate(outs):
        low = pl.multiple_of(2 * VROWS + first * AROWS, 16)
        out[pl.ds(low, 2 * AROWS), :] = audio

        @pl.when(step == dx)
        def _(out=out):
            for side in range(2):
                out[side * VROWS : (side + 1) * VROWS, :] = video[side]


def attend(chip, scalars, key_rows, qkv):
    message = jax.ShapeDtypeStruct((MESSAGE, HEAD_DIM), jnp.bfloat16)
    return pl.pallas_call(
        attend_kernel,
        grid_spec=pltpu.PrefetchScalarGridSpec(
            num_scalar_prefetch=2,
            grid=(XS,),
            in_specs=[
                pl.BlockSpec((2, KEYS), lambda i, c, s: (0, 0)),
                pl.BlockSpec((2, ROWS, HEAD_DIM), lambda i, c, s: (lax.rem(c[0] + i, XS), 0, 0)),
                pl.BlockSpec((GROUPS, ROWS, HEAD_DIM), lambda i, c, s: (0, 0, 1)),
                pl.BlockSpec((GROUPS, ROWS, HEAD_DIM), lambda i, c, s: (0, 0, 2)),
            ],
            out_specs=[pl.BlockSpec((MESSAGE, HEAD_DIM), lambda i, c, s: (0, 0))] * XS,
            scratch_shapes=[pltpu.VMEM((KEYS, 2 * HEAD_DIM), jnp.bfloat16)],
        ),
        out_shape=[message] * XS,
        compiler_params=pltpu.CompilerParams(vmem_limit_bytes=VMEM),
        cost_estimate=pl.CostEstimate(flops=0, bytes_accessed=1_000_000, transcendentals=0),
    )(chip, scalars, key_rows, qkv, qkv, qkv)


def gather_kernel(place, *refs):
    sources, video, audio = refs[: 2 * XS], refs[2 * XS], refs[2 * XS + 1]
    for number, source in enumerate(sources):
        head, dx = divmod(number, XS)
        lanes = pl.ds(dx * 256 + head * HEAD_DIM, HEAD_DIM)
        for half in range(2):
            side = place[1] if half == 0 else 1 - place[1]
            low = pl.multiple_of(side * VROWS, 32)
            video[half * VROWS : (half + 1) * VROWS, lanes] = source[pl.ds(low, VROWS), :]
        low = lax.rem(place[0] - dx + XS, XS) * 256 + head * HEAD_DIM
        audio[:, pl.ds(pl.multiple_of(low, HEAD_DIM), HEAD_DIM)] = source[2 * VROWS :, :]


def gather_rows(place, sources):
    whole = pl.BlockSpec(memory_space=pltpu.VMEM)
    return pl.pallas_call(
        gather_kernel,
        in_specs=[pl.BlockSpec(memory_space=pltpu.SMEM)] + [whole] * (2 * XS),
        out_specs=[whole, whole],
        out_shape=[
            jax.ShapeDtypeStruct((2 * VROWS, XS * 256), jnp.bfloat16),
            jax.ShapeDtypeStruct((GROUPS * AROWS, XS * 256), jnp.bfloat16),
        ],
        compiler_params=pltpu.CompilerParams(vmem_limit_bytes=VMEM),
        cost_estimate=pl.CostEstimate(flops=0, bytes_accessed=4_000_000, transcendentals=0),
    )(place, *sources)


def audio_kernel(left, weight, out):
    columns = out.shape[2]
    rows = [weight[x * ZS : (x + 1) * ZS, 0].reshape(columns, 256) for x in range(XS)]
    total = inner(left[...], jnp.concatenate(rows, axis=1))
    for device in range(GROUPS):
        out[device] = total[device * AROWS : device * AROWS + AUD].astype(jnp.bfloat16)


def project_audio(left, weights):
    blocks, slots, width, _ = weights.shape
    out = (GROUPS, AUD, ZS * width)
    return pl.pallas_call(
        audio_kernel,
        grid=(1,),
        in_specs=[
            pl.BlockSpec(left.shape, lambda n: (0, 0)),
            pl.BlockSpec((blocks, 1, width, 256), lambda n: (0, slots - 1, 0, 0)),
        ],
        out_specs=pl.BlockSpec(out, lambda n: (0, 0, 0)),
        out_shape=jax.ShapeDtypeStruct(out, jnp.bfloat16),
        compiler_params=pltpu.CompilerParams(vmem_limit_bytes=VMEM),
        cost_estimate=pl.CostEstimate(flops=0, bytes_accessed=8_000_000, transcendentals=0),
    )(left, weights)


def project_kernel(left, weight, own, other):
    columns = own.shape[1]
    rows = [weight[:, dx].reshape(columns, 256) for dx in range(XS)]
    total = inner(left[...], jnp.concatenate(rows, axis=1))
    own[...] = total[:VROWS].astype(jnp.bfloat16)
    other[...] = total[VROWS:].astype(jnp.bfloat16)


def project(left, weights):
    width = weights.shape[2]
    step, count = 2 * ZS, YS // 2
    out = pl.BlockSpec((VROWS, step * width), lambda n: (0, n))
    shape = jax.ShapeDtypeStruct((VROWS, count * step * width), jnp.bfloat16)
    return pl.pallas_call(
        project_kernel,
        grid=(count,),
        in_specs=[
            pl.BlockSpec(left.shape, lambda n: (0, 0)),
            pl.BlockSpec((step, XS, width, 256), lambda n: (n, 0, 0, 0)),
        ],
        out_specs=[out, out],
        out_shape=[shape, shape],
        compiler_params=pltpu.CompilerParams(vmem_limit_bytes=VMEM),
        cost_estimate=pl.CostEstimate(flops=0, bytes_accessed=8_000_000, transcendentals=0),
    )(left, weights)


def along(array, axis, shift):
    if axis == "x":
        return lax.ppermute(array, "uly", [(i, (i + 2 * shift) % GROUPS) for i in range(GROUPS)])
    pairs = []
    for i in range(YS * ZS):
        row, column = divmod(i, ZS)
        if axis == "y":
            row = (row + shift) % YS
        else:
            column = (column + shift) % ZS
        pairs.append((i, row * ZS + column))
    return lax.ppermute(array, "dp", pairs)


def after(array, *others):
    return lax.optimization_barrier((array, *others))[0]


def video_kernel(own, other, x, gate, out):
    total = own[...].astype(jnp.float32) + other[...].astype(jnp.float32)
    out[0] = (x[0].astype(jnp.float32) + gate[...] * total[:VID]).astype(jnp.bfloat16)


def finish_video(own, other, x, gate):
    total = own.shape[1]
    step = total // 2
    half = pl.BlockSpec((VROWS, step), lambda n: (0, n))
    video = pl.BlockSpec((1, VID, step), lambda n: (0, 0, n))
    return pl.pallas_call(
        video_kernel,
        grid=(2,),
        in_specs=[half, half, video, pl.BlockSpec((1, step), lambda n: (0, n))],
        out_specs=video,
        out_shape=jax.ShapeDtypeStruct(x.shape, jnp.bfloat16),
        compiler_params=pltpu.CompilerParams(vmem_limit_bytes=VMEM // 4),
        cost_estimate=pl.CostEstimate(flops=0, bytes_accessed=6_000_000, transcendentals=0),
    )(own, other, x, gate)


def place_kernel(parts, x, gate, out):
    quarters = []
    for chip in range(XS):
        pair = parts[2 * chip].astype(jnp.float32) + parts[2 * chip + 1].astype(jnp.float32)
        quarters.append(pair)
    total = jnp.concatenate(quarters, axis=1)
    out[0] = (x[0].astype(jnp.float32) + gate[...] * total).astype(jnp.bfloat16)


def finish_audio(parts, x, gate):
    return pl.pallas_call(
        place_kernel,
        out_shape=jax.ShapeDtypeStruct(x.shape, jnp.bfloat16),
        compiler_params=pltpu.CompilerParams(vmem_limit_bytes=VMEM // 4),
        cost_estimate=pl.CostEstimate(flops=0, bytes_accessed=3_000_000, transcendentals=0),
    )(parts, x, gate)


def timestep_embed(step_time):
    half = FREQ // 2
    index = jnp.arange(half, dtype=jnp.float32)
    freqs = jnp.exp(-math.log(10000.0) * index / half)
    angles = step_time * freqs
    return jnp.concatenate([jnp.cos(angles), jnp.sin(angles)]).astype(jnp.bfloat16)


def key_table(offset):
    index = jnp.arange(KEYS, dtype=jnp.int32)
    block, row = index // ROWS, index % ROWS
    is_video = row < VROWS
    video_time = (block // (GROUPS // 2)).astype(jnp.float32)
    audio_time = (block * AUD + (row - VROWS) + offset).astype(jnp.float32) / AUD_FRAME
    filling = (is_video & (row >= VID)) | (row >= VROWS + AUD)
    return jnp.stack(
        [jnp.where(is_video, video_time, audio_time), jnp.where(filling, OUTSIDE, 0.0)]
    ).astype(jnp.float32)


def shards(
    q_video,
    k_video,
    v_video,
    q_audio,
    k_audio,
    v_audio,
    x_video,
    x_audio,
    out_video_w,
    out_audio_w,
    mod_video,
    mod_audio,
    slopes,
    timesteps,
    pair_ids,
    offsets,
):
    position = lax.axis_index("uly")
    outer = lax.axis_index("dp")
    core = (position % 2).astype(jnp.int32)
    chip = (position // 2).astype(jnp.int32)
    own_heads = HEADS // GROUPS
    swap = [(i, i ^ 1) for i in range(GROUPS)]
    shifts = (1, 2, -1)

    block = out_video_w.T
    near = [along(block, "x", shift) for shift in shifts]
    moves = []
    for over in range(YS * ZS):
        row, column = divmod(over, ZS)
        for group in range(GROUPS):
            target = (group // 2 * ZS + column) * GROUPS + row * 2 + group % 2
            moves.append((over * GROUPS + group, target))
    block_a = lax.ppermute(out_audio_w.T, ("dp", "uly"), moves)
    packed = pack((q_video, k_video, v_video, q_audio, k_audio, v_audio))
    block, *near = lax.optimization_barrier((block, *near, packed[0]))[:-1]
    weights = lax.all_gather(jnp.stack([block, *near, block_a]), "dp", axis=0, tiled=False)

    qkv = [None, None]
    qkv[0] = lax.all_to_all(packed[0], "uly", split_axis=0, concat_axis=0, tiled=True)

    pair_count = timesteps.shape[0]
    step_time = jnp.sum(
        jnp.where(jnp.arange(pair_count, dtype=jnp.int32) == pair_ids[0], timesteps, 0)
    ).astype(jnp.float32)
    embed = timestep_embed(step_time)[None, :]
    gate_v = jnp.dot(embed, mod_video, preferred_element_type=jnp.float32)
    gate_a = jnp.dot(embed, mod_audio, preferred_element_type=jnp.float32)
    key_rows = key_table(offsets[0])
    offset = offsets[0].astype(jnp.float32)

    def attention(head, qkv):
        scalars = jnp.stack([slopes[position * own_heads + head], offset])
        messages = attend(chip[None], scalars, key_rows, qkv)
        sent = [along(array, "x", dx) if dx else array for dx, array in enumerate(messages)]
        return sent, messages[0]

    first, gate_v, gate_a, key_rows = lax.optimization_barrier((qkv[0], gate_v, gate_a, key_rows))
    qkv[1] = lax.all_to_all(
        after(packed[1], first), "uly", split_axis=0, concat_axis=0, tiled=True
    )
    sent0, done = attention(0, first)
    sent1, _ = attention(1, after(qkv[1], done))
    place = jnp.stack([chip, core])
    left_v, left_a = gather_rows(place, sent0 + sent1)
    parts = project_audio(left_a, weights)
    left_v = after(left_v, parts)
    parts = lax.all_to_all(parts, "uly", split_axis=0, concat_axis=0, tiled=True)
    own, other = project(left_v, weights)
    other, parts = lax.optimization_barrier((other, parts))
    received = lax.ppermute(other, "uly", swap)
    out_audio = finish_audio(parts, x_audio, gate_a)
    return finish_video(own, received, x_video, gate_v), out_audio


def solution(mesh):
    tokens = P("dp", "uly", None)
    return jax.shard_map(
        shards,
        mesh=mesh,
        in_specs=(tokens,) * 8 + (P("uly", "dp"), P("uly", "dp")) + (P(),) * 4 + (P("dp"), P("dp")),
        out_specs=(tokens, tokens),
        check_vma=False,
    )
```
